128 devices in a mesh: sfc: 8 (over x, core), blk: 16 (over y, z).
Axes of the slice: x: 4, y: 4, z: 4, core: 2. Of those that a mesh axis runs over, the one named last changes fastest.
Arguments:
- xin: bfloat16 [2048, 16, 1024], P(('sfc', 'blk')), may hold values from -6 to 6
- send_slot: int32 [128, 128], P(('sfc', 'blk')), may hold values from 0 to 15
- near_blocks: bfloat16 [256, 1024, 1024], P(('sfc', 'blk')), may hold values from -0.1875 to 0.1875
- near_row: int32 [256], P(('sfc', 'blk')), may hold values from 0 to 255, as said below
- near_src: int32 [256], P(('sfc', 'blk')), may hold values from 0 to 127, as said below
- far_left: bfloat16 [19968, 32, 1024], P(('sfc', 'blk')), may hold values from -0.3125 to 0.3125
- far_right: bfloat16 [19968, 32, 1024], P(('sfc', 'blk')), may hold values from -0.1875 to 0.1875
- far_row: int32 [19968], P(('sfc', 'blk')), may hold values from 0 to 255, as said below
- far_src: int32 [19968], P(('sfc', 'blk')), may hold values from 0 to 127, as said below
Outputs:
- product: float32 [2048, 16, 1024], P(('sfc', 'blk'))
The draws below stay inside these ranges and needn't reach their ends.
Inputs may be any that keep to these rules, and one draw needn't show every extreme that they name: On every device, its 2 near_src entries are the device itself and another device of its cluster group, and near_src and far_src together name every device at least once. `far_src`: see near_src. On every device, the output clusters of its blocks (near_row and far_row together) are exactly 8 of the 16 clusters of each device of its cluster group. `far_row`: see near_row.
All inputs are finite; a program needn't handle non-finite values.
Results may differ from the reference program's by a relative error of at most 0.0027.
Values may be sent and summed in bfloat16 or wider, within the bound.
A program may use at most 128 MiB of HBM per device.

```python
import jax
import jax.numpy as jnp
from jax import lax

LEAF = 1024
RANK = 32
NRHS = 16
CL_DEV = 16
NEAR_DEV = 2
FAR_DEV = 156
NC = 2048
GROUP = 256
ROWS_PEER = 8
NEAR = 256
FAR = 19968
N_SFC = 8
N_BLK = 16
DEVICES = 128


def owner_one(key, device):
    keys = jax.random.split(key, 5)
    group = device // N_BLK
    member = device % N_BLK
    other = group * N_BLK + (member + jax.random.randint(keys[0], (), 1, N_BLK)) % N_BLK
    order = jax.random.permutation(keys[1], DEVICES).astype(jnp.int32)
    taken = (order == device) | (order == other)
    score = jnp.where(taken, DEVICES + jnp.arange(DEVICES, dtype=jnp.int32), jnp.arange(DEVICES, dtype=jnp.int32))
    remain = order[jnp.argsort(score)][:DEVICES - NEAR_DEV]
    extra = FAR_DEV - (DEVICES - NEAR_DEV)
    offset = jax.random.randint(keys[2], (extra,), -1, 2)
    within = jax.random.randint(keys[3], (extra,), 0, N_BLK)
    repeats = ((group + offset) % N_SFC * N_BLK + within).astype(jnp.int32)
    far_list = jnp.concatenate([remain, repeats])
    far_list = far_list[jax.random.permutation(keys[4], FAR_DEV)]
    near_list = jnp.stack([device, other]).astype(jnp.int32)
    return (near_list, far_list)


def owner_lists(key):
    keys = jax.random.split(key, DEVICES)
    return jax.vmap(owner_one)(keys, jnp.arange(DEVICES, dtype=jnp.int32))


def rows_one(key):
    keys = jax.random.split(key, 3)
    peer_keys = jax.random.split(keys[0], N_BLK)
    picks = jax.vmap(lambda k: jax.random.permutation(k, CL_DEV)[:ROWS_PEER])(peer_keys)
    chosen = (picks + jnp.arange(N_BLK)[:, None] * CL_DEV).reshape(-1).astype(jnp.int32)
    count = N_BLK * ROWS_PEER
    total = NEAR_DEV + FAR_DEV
    extra = jax.random.randint(keys[1], (total - count,), 0, count)
    rows = jnp.concatenate([chosen, chosen[extra]])
    return rows[jax.random.permutation(keys[2], total)].astype(jnp.int32)


def row_lists(key):
    keys = jax.random.split(key, DEVICES)
    return jax.vmap(rows_one)(keys)


def draw_near_src(key, part):
    return owner_lists(key)[0].reshape(-1)


def draw_far_src(key, part):
    return owner_lists(key)[1].reshape(-1)


def draw_near_row(key, part):
    return row_lists(key)[:, :NEAR_DEV].reshape(-1)


def draw_far_row(key, part):
    return row_lists(key)[:, NEAR_DEV:].reshape(-1)


def touch_ends(entries, stream_key, smallest, high):
    place = [jax.random.randint(jax.random.fold_in(stream_key, axis), (), 0, length) for axis, length in enumerate(entries.shape)]
    longest = entries.shape.index(max(entries.shape))
    beside = place[:longest] + [(place[longest] + 1) % entries.shape[longest]] + place[longest + 1:]
    return entries.at[tuple(place)].set(smallest).at[tuple(beside)].set(high)


def shard_levels(stream_key, extent, pieces, least, high):
    loudness, own = 1.0, jax.random.fold_in(stream_key, 6)
    for dim, blocks in pieces:
        steps = jnp.exp(jax.random.uniform(jax.random.fold_in(own, dim), (blocks,), jnp.float32, least / len(pieces), high / len(pieces)))
        loudness = loudness * jnp.repeat(steps, extent[dim] // blocks).reshape([-1 if axis == dim else 1 for axis in range(len(extent))])
    return loudness


def noise(stream_key, extent, spread, reach, shards=(), kind=jnp.bfloat16):
    gain = shard_levels(stream_key, extent, shards, -0.22, 0.18) if shards else 1.0
    drawn = jax.random.normal(stream_key, extent, jnp.float32) * spread * gain
    return jnp.minimum(jnp.maximum(drawn, -reach), reach).astype(kind)


def setup_inputs(seed: int = 0) -> dict:
    seeds = jax.random.split(jax.random.key(seed), 10)
    xin = noise(seeds[0], (NC, NRHS, LEAF), 1.0, 6.0, ((0, 128),))
    send_slot = touch_ends(jax.random.randint(seeds[1], (DEVICES, DEVICES), 0, CL_DEV), jax.random.fold_in(seeds[1], 1), 0, CL_DEV - 1).astype(jnp.int32)
    near_blocks = noise(seeds[2], (NEAR, LEAF, LEAF), LEAF ** -0.5, 0.1875, ((0, 128),))
    near_row = draw_near_row(jax.random.fold_in(seeds[9], 71), 0)
    near_src = draw_near_src(jax.random.fold_in(seeds[9], 71), 0)
    far_left = noise(seeds[5], (FAR, RANK, LEAF), (RANK * FAR_DEV // CL_DEV) ** -0.5, 0.3125, ((0, 128),))
    far_right = noise(seeds[6], (FAR, RANK, LEAF), LEAF ** -0.5, 0.1875, ((0, 128),))
    far_row = draw_far_row(jax.random.fold_in(seeds[9], 71), 0)
    far_src = draw_far_src(jax.random.fold_in(seeds[9], 71), 0)
    return {"xin": xin, "send_slot": send_slot, "near_blocks": near_blocks, "near_row": near_row, "near_src": near_src, "far_left": far_left, "far_right": far_right, "far_row": far_row, "far_src": far_src}


def reference(xin, send_slot, near_blocks, near_row, near_src, far_left, far_right, far_row, far_src):
    near_dev = jnp.arange(NEAR, dtype=jnp.int32) // NEAR_DEV
    far_dev = jnp.arange(FAR, dtype=jnp.int32) // FAR_DEV
    near_col = near_src * CL_DEV + send_slot[near_src, near_dev]
    far_col = far_src * CL_DEV + send_slot[far_src, far_dev]
    near_out = (near_dev // N_BLK) * GROUP + near_row
    far_out = (far_dev // N_BLK) * GROUP + far_row
    product = jnp.zeros((NC, NRHS, LEAF), jnp.float32)

    def step(device, total):
        lo = (device * NEAR_DEV).astype(jnp.int32)
        blocks = lax.dynamic_slice_in_dim(near_blocks, lo, NEAR_DEV, 0)
        cols = lax.dynamic_slice_in_dim(near_col, lo, NEAR_DEV, 0)
        outs = lax.dynamic_slice_in_dim(near_out, lo, NEAR_DEV, 0)
        inputs = xin[cols].astype(jnp.float32)
        near_term = jnp.einsum('bij,brj->bri', blocks.astype(jnp.float32), inputs)
        total = total.at[outs].add(near_term)
        fo = (device * FAR_DEV).astype(jnp.int32)
        left = lax.dynamic_slice_in_dim(far_left, fo, FAR_DEV, 0).astype(jnp.float32)
        right = lax.dynamic_slice_in_dim(far_right, fo, FAR_DEV, 0).astype(jnp.float32)
        fcols = lax.dynamic_slice_in_dim(far_col, fo, FAR_DEV, 0)
        fouts = lax.dynamic_slice_in_dim(far_out, fo, FAR_DEV, 0)
        finputs = xin[fcols].astype(jnp.float32)
        projection = jnp.einsum('bkj,brj->brk', right, finputs).astype(jnp.bfloat16)
        far_term = jnp.einsum('bki,brk->bri', left, projection.astype(jnp.float32))
        return total.at[fouts].add(far_term)

    return lax.fori_loop(0, DEVICES, step, product)
```

```python
import functools

import jax
import jax.numpy as jnp
from jax import lax
from jax.experimental import pallas as pl
from jax.experimental.pallas import tpu as pltpu
from jax.sharding import PartitionSpec as P

MESH = pl.DeviceIdType.MESH
BF = jnp.bfloat16
F32 = jnp.float32
I32 = jnp.int32
CL, RHS, LEAF, RANK = 16, 16, 1024, 32
NEAR, FAR, SLOTS = 2, 156, 8
ALL = NEAR + FAR
PAD = 160
HALF = LEAF // 2
COLS = ((0, 384), (384, 384), (768, 256))
ORDER = ((0, 1, 2), (1, 2, 0), (2, 0, 1))
FIRST = (1, 2)
SECOND = (2, 1)


def kernel(
    xin, slots_in, near_row, near_src, far_row, far_src, near_hbm, left_hbm, right_hbm,
    out,
    g0, g1, g2, slot_v, slot_s, t0, t1, t2, m0, m1, m2, inc,
    near, left, right, keys, tab_v, tab_s, inv_v, inv_r, inv_s,
    proj, term, cum, send0, send1, recv0, recv1, fold0, fold1, last0, last1,
    wsem, csem, s1s, s1r, sls, slr, s2s, s2r, s3s, s3r, ivs, ivr, o1s, o1r, o2s, o2r,
):
    sfc, blk = lax.axis_index("sfc"), lax.axis_index("blk")
    core = sfc % 2
    pos = (sfc // 2, blk // 4, blk % 4)

    def device(axis, where, flip=0):
        p = list(pos)
        p[axis] = where
        return (p[0] * 2 + (core + flip) % 2, p[1] * 4 + p[2])

    def ahead(axis, d):
        return (pos[axis] + d) % 4

    def remote(src, dst, ssem, rsem, to):
        return pltpu.make_async_remote_copy(
            src_ref=src, dst_ref=dst, send_sem=ssem, recv_sem=rsem, device_id=to, device_id_type=MESH
        )

    weights = [
        pltpu.make_async_copy(near_hbm, near, wsem.at[0]),
        pltpu.make_async_copy(right_hbm, right.at[pl.ds(0, FAR)], wsem.at[1]),
        pltpu.make_async_copy(left_hbm, left.at[pl.ds(0, FAR)], wsem.at[2]),
    ]

    barrier = pltpu.get_barrier_semaphore()
    peers = [device(0, pos[0], 1)]
    for axis in range(3):
        for d in range(1, 4):
            for flip in range(2):
                peers.append(device(axis, ahead(axis, d), flip))
    for to in peers:
        pl.semaphore_signal(barrier, inc=1, device_id=to, device_id_type=MESH)
    pl.semaphore_wait(barrier, len(peers))

    got = (g0, g1, g2)
    stage1, local1 = [], []
    for k in range(3):
        first = ORDER[k][0]
        lo, wide = COLS[k]
        part = xin.at[:, :, pl.ds(lo, wide)]
        mine = got[k].at[pos[first]]
        sends = []
        for d in range(1, 4):
            to = device(first, ahead(first, d))
            a = remote(slots_in, slot_v.at[k, pos[first]], sls.at[k, d - 1], slr.at[k, d - 1], to)
            b = remote(part, mine, s1s.at[k, d - 1], s1r.at[k, d - 1], to)
            a.start()
            b.start()
            sends += [a, b]
        own = [
            pltpu.make_async_copy(slots_in, slot_v.at[k, pos[first]], csem.at[2 * k]),
            pltpu.make_async_copy(part, mine, csem.at[2 * k + 1]),
        ]
        for c in own:
            c.start()
        stage1.append(sends)
        local1.append(own)
    for c in weights:
        c.start()

    right[FAR:PAD] = jnp.zeros((PAD - FAR, RANK, LEAF), BF)
    left[FAR:PAD] = jnp.zeros((PAD - FAR, RANK, LEAF), BF)

    def fill_far(j, _):
        keys[pl.ds(j, 1), :] = jnp.full((1, 256), far_row[j], I32)
        return 0

    lax.fori_loop(0, FAR, fill_far, 0)
    for j in range(NEAR):
        keys[FAR + j : FAR + j + 1, :] = jnp.full((1, 256), near_row[j], I32)
    keys[ALL:PAD, :] = jnp.full((PAD - ALL, 256), 300, I32)
    row_c = keys[...]
    down = lax.broadcasted_iota(I32, (PAD, 256), 0)
    lane = lax.broadcasted_iota(I32, (PAD, 256), 1)
    row_r = jnp.sum(jnp.where(down == lane, row_c, 0), axis=0, keepdims=True)
    real = lane < PAD
    same = real & (row_r == row_c)
    less = real & (row_r < row_c)
    first_r = jnp.sum(jnp.where(same & (down < lane), 1, 0), axis=0, keepdims=True) == 0
    place = jnp.sum(jnp.where(less | (same & (lane < down)), 1, 0), axis=1, keepdims=True)
    final = jnp.sum(jnp.where(less | same, 1, 0), axis=1, keepdims=True) - 1
    slot = jnp.sum(jnp.where(less & first_r, 1, 0), axis=1, keepdims=True)
    here = place == lane
    order = jnp.sum(jnp.where(here, down, 0), axis=0, keepdims=True)
    sorted_row = jnp.sum(jnp.where(here, row_c, 0), axis=0, keepdims=True)
    ends = jnp.max(jnp.where(slot == lane, final, 0), axis=0, keepdims=True)
    seat = jnp.max(jnp.where(row_c == lane, 8 - (slot & 7), 0), axis=0, keepdims=True)
    tab_v[0:1, :] = order
    tab_v[1:2, :] = sorted_row
    tab_v[2:3, :] = ends
    inv_v[0:1, :] = 8 - seat
    tab_copy = pltpu.make_async_copy(tab_v, tab_s, csem.at[6])
    tab_copy.start()
    places = []
    for h in range(2):
        axis = FIRST[h]
        for d in range(1, 4):
            c = remote(inv_v, inv_r.at[h, pos[axis]], ivs.at[h, d - 1], ivr.at[h, d - 1], device(axis, ahead(axis, d)))
            c.start()
            places.append(c)
        c = pltpu.make_async_copy(inv_v, inv_r.at[h, pos[axis]], csem.at[7 + h])
        c.start()
        places.append(c)
    recv = (recv0, recv1)
    for h in range(2):
        recv[h][:, :, SLOTS] = jnp.zeros((4, 4, RHS, HALF), BF)

    pick, mid = (t0, t1, t2), (m0, m1, m2)
    stage2 = []
    for k in (2, 0, 1):
        _, second, third = ORDER[k]
        for c in stage1[k]:
            c.wait_recv()
        for c in local1[k]:
            c.wait()
        copy = pltpu.make_async_copy(slot_v.at[k], slot_s.at[k], csem.at[9 + k])
        copy.start()
        copy.wait()

        def chosen(i, there, k=k, second=second, third=third):
            a, c, co = i // 8, (i // 2) % 4, i % 2
            p = list(pos)
            p[second] = there
            p[third] = c
            where = (p[0] * 2 + co) * 16 + p[1] * 4 + p[2]
            return a, c, co, got[k][a, slot_s[k, a, 0, where]]

        for d in range(1, 4):
            there = ahead(second, d)

            def put(i, _, k=k, d=d, there=there, chosen=chosen):
                a, c, co, value = chosen(i, there)
                pick[k][d - 1, a, c, co] = value
                return 0

            lax.fori_loop(0, 32, put, 0, unroll=4)
            dst = mid[k].at[pos[second]] if k == 2 else mid[k].at[:, pos[second]]
            c = remote(pick[k].at[d - 1], dst, s2s.at[k, d - 1], s2r.at[k, d - 1], device(second, there))
            c.start()
            stage2.append((k, c))

        def keep(i, _, k=k, second=second, chosen=chosen):
            a, c, co, value = chosen(i, pos[second])
            if k == 2:
                mid[k][pos[second], a, c, co] = value
            else:
                mid[k][a, pos[second], c, co] = value
            return 0

        lax.fori_loop(0, 32, keep, 0, unroll=4)

    stage3, local3 = [], []
    for k in (2, 0, 1):
        third = ORDER[k][2]
        lo, wide = COLS[k]
        for kk, c in stage2:
            if kk == k:
                c.wait_recv()
        cols = pl.ds(lo, wide)
        if k == 0:
            dst = inc.at[:, core, :, pos[2], :, cols]
        elif k == 1:
            dst = inc.at[pos[0], core, :, :, :, cols]
        else:
            dst = inc.at[:, core, pos[1], :, :, cols]
        for d in (1, 3, 2, 0):
            there = ahead(third, d)
            for flip in range(2):
                src = mid[k].at[:, :, there, (core + flip) % 2]
                if d == 0 and flip == 0:
                    c = pltpu.make_async_copy(src, dst, csem.at[12 + k])
                    local3.append(c)
                else:
                    n = d * 2 + flip - 1
                    c = remote(src, dst, s3s.at[k, n], s3r.at[k, n], device(third, there, flip))
                    stage3.append(c)
                c.start()
    tab_copy.wait()
    for c in weights:
        c.wait()
    for c in stage3:
        c.wait_recv()
    for c in local3:
        c.wait()

    def cluster(s):
        return inc[s >> 5, (s >> 4) & 1, (s >> 2) & 3, s & 3]

    diag = lax.broadcasted_iota(I32, (128, 256), 0) // 16 == lax.broadcasted_iota(I32, (128, 256), 1) // 32

    def project(g, _):
        x = jnp.concatenate([cluster(far_src[jnp.minimum(8 * g + e, FAR - 1)]) for e in range(8)], axis=0)
        w = right[pl.ds(8 * g, 8)].reshape(256, LEAF)
        r = lax.dot_general(x, w, (((1,), (1,)), ((), ())), preferred_element_type=F32)
        proj[g] = jnp.where(diag, r, 0.0).astype(BF)
        return 0

    lax.fori_loop(0, PAD // 8, project, 0)

    send = (send0, send1)
    out1 = []
    for h in range(2):
        first, second = FIRST[h], SECOND[h]
        cols = pl.ds(HALF * h, HALF)

        def far(g, _, cols=cols):
            w = left[pl.ds(8 * g, 8), :, cols].reshape(256, HALF)
            t = jnp.dot(proj[g], w, preferred_element_type=F32)
            term[pl.ds(8 * g, 8)] = t.reshape(8, RHS, HALF)
            return 0

        lax.fori_loop(0, PAD // 8, far, 0)
        for n in range(NEAR):
            w = near[n, HALF * h : HALF * (h + 1), :]
            term[FAR + n] = lax.dot_general(
                cluster(near_src[n]), w, (((1,), (1,)), ((), ())), preferred_element_type=F32
            )

        def scan(q, carry):
            value, before = carry
            row = tab_s[1, q]
            keep = (row == before).astype(F32)
            value = value * keep + term[tab_s[0, q]]
            cum[q] = value.astype(BF)
            return value, row

        lax.fori_loop(0, ALL, scan, (jnp.zeros((RHS, HALF), F32), jnp.int32(-1)), unroll=2)

        for d in (1, 3, 2, 0):
            there = ahead(first, d)

            def load(i, _, h=h, there=there):
                w, t = i // 8, i % 8
                p = there * 4 + w if h == 0 else w * 4 + there
                value = cum[tab_s[2, p * 8 + t]]
                if d == 0:
                    recv[h][there, w, t] = value
                else:
                    send[h][d - 1, w, t] = value
                return 0

            lax.fori_loop(0, 32, load, 0, unroll=4)
            if d:
                c = remote(
                    send[h].at[d - 1], recv[h].at[pos[first], :, pl.ds(0, SLOTS)],
                    o1s.at[h, d - 1], o1r.at[h, d - 1], device(first, there),
                )
                c.start()
                out1.append((h, c))

    for c in places:
        c.wait()
    inv_copy = pltpu.make_async_copy(inv_r, inv_s, csem.at[15])
    inv_copy.start()
    inv_copy.wait()

    fold, last = (fold0, fold1), (last0, last1)
    out2 = []
    for h in range(2):
        first, second = FIRST[h], SECOND[h]
        for hh, c in out1:
            if hh == h:
                c.wait_recv()
        for d in (1, 3, 2, 0):
            there = ahead(second, d)
            p = pos[first] * 4 + there if h == 0 else there * 4 + pos[first]

            def add(r, _, h=h, there=there, p=p, d=d):
                total = recv[h][0, there, inv_s[h, 0, 0, p * 16 + r]].astype(F32)
                for s in range(1, 4):
                    total += recv[h][s, there, inv_s[h, s, 0, p * 16 + r]].astype(F32)
                if d == 0:
                    out[r, :, HALF * h : HALF * (h + 1)] = total
                else:
                    fold[h][d - 1, r] = total.astype(BF)
                return 0

            lax.fori_loop(0, CL, add, 0, unroll=2)
            if d:
                c = remote(
                    fold[h].at[d - 1], last[h].at[d - 1],
                    o2s.at[h, d - 1], o2r.at[h, d - 1], device(second, there),
                )
                c.start()
                out2.append((h, c))
    for h in range(2):
        for hh, c in out2:
            if hh == h:
                c.wait_recv()

        def finish(r, _, h=h):
            cols = slice(HALF * h, HALF * (h + 1))
            total = out[r, :, cols]
            for s in range(3):
                total += last[h][s, r].astype(F32)
            out[r, :, cols] = total
            return 0

        lax.fori_loop(0, CL, finish, 0, unroll=2)

    for c in sum(stage1, []) + [c for _, c in stage2 + out1 + out2] + stage3:
        c.wait_send()


def local(xin, send_slot, near_blocks, near_row, near_src, far_left, far_right, far_row, far_src):
    vmem, smem = pl.BlockSpec(memory_space=pltpu.VMEM), pl.BlockSpec(memory_space=pltpu.SMEM)
    hbm = pl.BlockSpec(memory_space=pl.ANY)
    widths = [w for _, w in COLS]
    dma = pltpu.SemaphoreType.DMA
    scratch = [pltpu.VMEM((4, CL, RHS, w), BF) for w in widths]
    scratch += [pltpu.VMEM((3, 4, 1, 128), I32), pltpu.SMEM((3, 4, 1, 128), I32)]
    scratch += [pltpu.VMEM((3, 4, 4, 2, RHS, w), BF) for w in widths]
    scratch += [pltpu.VMEM((4, 4, 4, 2, RHS, w), BF) for w in widths]
    scratch += [pltpu.VMEM((4, 2, 4, 4, RHS, LEAF), BF)]
    scratch += [
        pltpu.VMEM((NEAR, LEAF, LEAF), BF),
        pltpu.VMEM((PAD, RANK, LEAF), BF),
        pltpu.VMEM((PAD, RANK, LEAF), BF),
        pltpu.VMEM((PAD, 256), I32),
        pltpu.VMEM((8, 256), I32),
        pltpu.SMEM((8, 256), I32),
        pltpu.VMEM((1, 256), I32),
        pltpu.VMEM((2, 4, 1, 256), I32),
        pltpu.SMEM((2, 4, 1, 256), I32),
        pltpu.VMEM((PAD // 8, 128, 256), BF),
        pltpu.VMEM((PAD, RHS, HALF), F32),
        pltpu.VMEM((PAD, RHS, HALF), BF),
    ]
    scratch += [pltpu.VMEM((3, 4, SLOTS, RHS, HALF), BF)] * 2
    scratch += [pltpu.VMEM((4, 4, SLOTS + 1, RHS, HALF), BF)] * 2
    scratch += [pltpu.VMEM((3, CL, RHS, HALF), BF)] * 4
    scratch += [dma((3,)), dma((16,)), dma((3, 3)), dma((3, 3)), dma((3, 3)), dma((3, 3)), dma((3, 3)), dma((3, 3))]
    scratch += [dma((3, 7)), dma((3, 7))] + [dma((2, 3))] * 6
    return pl.pallas_call(
        kernel,
        out_shape=jax.ShapeDtypeStruct((CL, RHS, LEAF), F32),
        in_specs=[vmem, vmem, smem, smem, smem, smem, hbm, hbm, hbm],
        out_specs=vmem,
        scratch_shapes=scratch,
        compiler_params=pltpu.CompilerParams(
            collective_id=0, has_side_effects=True, vmem_limit_bytes=62 << 20
        ),
        cost_estimate=pl.CostEstimate(flops=800_000_000, bytes_accessed=26_000_000, transcendentals=0),
        name="hmatrix",
    )(xin, send_slot, near_row, near_src, far_row, far_src, near_blocks, far_left, far_right)


def solution(mesh):
    both = ("sfc", "blk")
    placed = (
        P(both, None, None), P(both, None), P(both, None, None), P(both), P(both),
        P(both, None, None), P(both, None, None), P(both), P(both),
    )
    return jax.shard_map(local, mesh=mesh, in_specs=placed, out_specs=P(both, None, None), check_vma=False)
```

```python
import functools

import jax
import jax.numpy as jnp
from jax import lax
from jax.experimental import pallas as pl
from jax.experimental.pallas import tpu as pltpu
from jax.sharding import PartitionSpec as P

MESH = pl.DeviceIdType.MESH
BF = jnp.bfloat16
F32 = jnp.float32
I32 = jnp.int32
CL, RHS, LEAF, RANK = 16, 16, 1024, 32
NEAR, FAR, SLOTS = 2, 156, 8
ALL = NEAR + FAR
PAD = 160
PARTS = 8
THIN = LEAF // PARTS
WIDE = 2 * THIN
COLS = ((0, 384), (384, 384), (768, 256))
ORDER = ((0, 1, 2), (1, 2, 0), (2, 0, 1))
AXES = ((1, 2), (2, 1))


def kernel(
    xin, slots_in, near_row_in, near_src_in, far_row_in, far_src_in, near_hbm, left_hbm, right_hbm,
    out,
    x_v, near_row, near_src, far_row, far_src, slot_v, slot_o, slot_s,
    g0, g1, g2, t0, t1, t2, m0, m1, m2, i0, i1, i2,
    near, left, right, keys, tab_v, tab_s, inv_v, inv_r, inv_s,
    sums, proj, term, cum, send, r0, r1, r2, r3, r4, r5, r6, r7, fold, last, out_v,
    wsem, csem, ksem, s1s, s1r, sls, slr, s2s, s2r, s3s, s3r, ivs, ivr, o1s, o1r, o2s, o2r, osem,
):
    sfc, blk = lax.axis_index("sfc"), lax.axis_index("blk")
    core = sfc % 2
    pos = (sfc // 2, blk // 4, blk % 4)

    def moved(steps, flip=0):
        p = [(pos[a] + steps.get(a, 0)) % 4 for a in range(3)]
        return p[0] * 2 + (core + flip) % 2, p[1] * 4 + p[2]

    def remote(src, dst, ssem, rsem, to):
        return pltpu.make_async_remote_copy(
            src_ref=src, dst_ref=dst, send_sem=ssem, recv_sem=rsem, device_id=to, device_id_type=MESH
        )

    def starts(*copies):
        for c in copies:
            c.start()
        return list(copies)

    barrier = pltpu.get_barrier_semaphore()
    peers = [moved({}, 1)] + [moved({a: d}, f) for a in range(3) for d in range(1, 4) for f in range(2)]
    for to in peers:
        pl.semaphore_signal(barrier, inc=1, device_id=to, device_id_type=MESH)
    own_x, own_slot = starts(
        pltpu.make_async_copy(xin, x_v, csem.at[0]),
        pltpu.make_async_copy(slots_in, slot_o, csem.at[1]),
    )
    index = starts(
        pltpu.make_async_copy(near_row_in, near_row, csem.at[2]),
        pltpu.make_async_copy(near_src_in, near_src, csem.at[3]),
        pltpu.make_async_copy(far_row_in, far_row, csem.at[4]),
        pltpu.make_async_copy(far_src_in, far_src, csem.at[5]),
    )
    right[FAR:PAD] = jnp.zeros((PAD - FAR, RANK, LEAF), BF)
    left[FAR:PAD] = jnp.zeros((PAD - FAR, RANK, LEAF), BF)

    recv = (r0, r1, r2, r3, r4, r5, r6, r7)

    def clear(i, _):
        for buffer in recv:
            buffer[i // 4, i % 4, SLOTS] = jnp.zeros((RHS, THIN), BF)
        return 0

    lax.fori_loop(0, 16, clear, 0)
    own_x.wait()
    own_slot.wait()
    pl.semaphore_wait(barrier, len(peers))

    got = (g0, g1, g2)
    stage1, slots1 = [[], [], []], []
    for k in range(3):
        for d in (1, 3, 2):
            to = moved({ORDER[k][0]: d})
            slots1 += starts(remote(slots_in, slot_v.at[k, 3 - d], sls.at[k, d - 1], slr.at[k, d - 1], to))
    for d in (1, 3, 2):
        for k in (0, 1, 2):
            lo, wide = COLS[k]
            stage1[k] += starts(remote(
                x_v.at[:, :, pl.ds(lo, wide)], got[k].at[3 - d],
                s1s.at[k, d - 1], s1r.at[k, d - 1], moved({ORDER[k][0]: d}),
            ))

    pick, mid = (t0, t1, t2), (m0, m1, m2)
    stage2 = [[], [], []]

    def wanted(k, a, c, f, d):
        where = moved({ORDER[k][1]: d, ORDER[k][2]: c}, f)
        return where[0] * 16 + where[1]

    def choose(k, d, lo, n, value):
        def put(i, _):
            a, c, f = lo + i // 8, (i // 2) % 4, i % 2
            v = value(k, a, c, f, d)
            if d:
                pick[k][d - 1, a, c, f] = v
            elif k == 2:
                mid[k][0, a, c, f] = v
            else:
                mid[k][a, 0, c, f] = v
            return 0

        lax.fori_loop(0, 8 * n, put, 0, unroll=8)

    def pass_on(k, d, lo, n):
        group = 0 if lo == 0 else 1
        dst = mid[k].at[4 - d, pl.ds(lo, n)] if k == 2 else mid[k].at[pl.ds(lo, n), 4 - d]
        stage2[k] += starts(remote(
            pick[k].at[d - 1, pl.ds(lo, n)], dst,
            s2s.at[k, group, d - 1], s2r.at[k, group, d - 1], moved({ORDER[k][1]: d}),
        ))

    def value_own(k, a, c, f, d):
        lo, wide = COLS[k]
        return x_v[slot_o[0, wanted(k, 0, c, f, d)], :, lo : lo + wide]

    def value_got(k, a, c, f, d):
        return got[k][a - 1, slot_s[k, a - 1, 0, wanted(k, a, c, f, d)]]

    for d in (1, 3, 2):
        for k in (0, 1, 2):
            choose(k, d, 0, 1, value_own)
            pass_on(k, d, 0, 1)
    for k in range(3):
        choose(k, 0, 0, 1, value_own)
    weights = starts(
        pltpu.make_async_copy(right_hbm, right.at[pl.ds(0, FAR)], wsem.at[0]),
        pltpu.make_async_copy(left_hbm, left.at[pl.ds(0, FAR)], wsem.at[1]),
        pltpu.make_async_copy(near_hbm, near, wsem.at[2]),
    )
    for c in slots1:
        c.wait_recv()
    (slot_copy,) = starts(pltpu.make_async_copy(slot_v, slot_s, csem.at[6]))

    for c in index:
        c.wait()

    def fill_far(j, _):
        keys[pl.ds(j, 1), :] = jnp.full((1, 256), far_row[j], I32)
        return 0

    lax.fori_loop(0, FAR, fill_far, 0, unroll=4)
    for j in range(NEAR):
        keys[FAR + j : FAR + j + 1, :] = jnp.full((1, 256), near_row[j], I32)
    keys[ALL:PAD, :] = jnp.full((PAD - ALL, 256), 300, I32)
    row_c = keys[...]
    down = lax.broadcasted_iota(I32, (PAD, 256), 0)
    lane = lax.broadcasted_iota(I32, (PAD, 256), 1)
    row_r = jnp.sum(jnp.where(down == lane, row_c, 0), axis=0, keepdims=True)
    real = lane < PAD
    same = real & (row_r == row_c)
    less = real & (row_r < row_c)
    first_r = jnp.sum(jnp.where(same & (down < lane), 1, 0), axis=0, keepdims=True) == 0
    place = jnp.sum(jnp.where(less | (same & (lane < down)), 1, 0), axis=1, keepdims=True)
    final = jnp.sum(jnp.where(less | same, 1, 0), axis=1, keepdims=True) - 1
    slot = jnp.sum(jnp.where(less & first_r, 1, 0), axis=1, keepdims=True)
    here = place == lane
    tab_v[0:1, :] = jnp.sum(jnp.where(here, down, 0), axis=0, keepdims=True)
    tab_v[1:2, :] = jnp.sum(jnp.where(here, row_c, 0), axis=0, keepdims=True)
    tab_v[2:3, :] = jnp.max(jnp.where(slot == lane, final, 0), axis=0, keepdims=True)
    seat = jnp.max(jnp.where(row_c == lane, 8 - (slot & 7), 0), axis=0, keepdims=True)
    inv_v[0:1, :] = 8 - seat
    (tab_copy,) = starts(pltpu.make_async_copy(tab_v, tab_s, csem.at[7]))
    places = []
    for h in range(2):
        for d in range(1, 4):
            places += starts(remote(
                inv_v, inv_r.at[h, 4 - d], ivs.at[h, d - 1], ivr.at[h, d - 1], moved({AXES[h][0]: d})
            ))
        places += starts(pltpu.make_async_copy(inv_v, inv_r.at[h, 0], csem.at[8 + h]))

    inc = (i0, i1, i2)

    stage3, own3 = [[], [], []], [[], [], []]

    def deliver(k, group):
        part = 0 if group == 0 else pl.ds(1, 3)
        for d in (1, 3, 2, 0):
            e = (4 - d) % 4
            for f in range(2):
                if k == 2:
                    src, dst = mid[k].at[part, :, d, f], inc[k].at[part, f, e]
                elif k == 1:
                    src, dst = mid[k].at[:, part, d, f], inc[k].at[e, f, :, part]
                else:
                    src, dst = mid[k].at[:, part, d, f], inc[k].at[:, f, part, e]
                if d == 0 and f == 0:
                    own3[k].extend(starts(pltpu.make_async_copy(src, dst, ksem.at[k, group])))
                else:
                    n = d * 2 + f - 1
                    stage3[k].extend(starts(remote(
                        src, dst, s3s.at[k, group, n], s3r.at[k, group, n], moved({ORDER[k][2]: d}, f)
                    )))

    slot_copy.wait()
    for k in (2, 1, 0):
        for c in stage1[k]:
            c.wait_recv()
        for d in (1, 3, 2):
            choose(k, d, 1, 3, value_got)
            pass_on(k, d, 1, 3)
    for k in (2, 1, 0):
        choose(k, 0, 1, 3, value_got)
        deliver(k, 0)
    for k in (2, 1, 0):
        for c in stage2[k]:
            c.wait_recv()
        deliver(k, 1)

    def cluster(s, k):
        return inc[k][
            ((s >> 5) - pos[0]) & 3, ((s >> 4) - core) & 1, ((s >> 2) - pos[1]) & 3, (s - pos[2]) & 3
        ]

    diag = lax.broadcasted_iota(I32, (128, 256), 0) // 16 == lax.broadcasted_iota(I32, (128, 256), 1) // 32
    for c in weights:
        c.wait()
    for k in (2, 1, 0):
        for c in stage3[k]:
            c.wait_recv()
        for c in own3[k]:
            c.wait()

        def project(g, _, k=k):
            lo, wide = COLS[k]
            x = jnp.concatenate([cluster(far_src[jnp.minimum(8 * g + e, FAR - 1)], k) for e in range(8)], axis=0)
            w = right[pl.ds(8 * g, 8), :, lo : lo + wide].reshape(256, wide)
            r = lax.dot_general(x, w, (((1,), (1,)), ((), ())), preferred_element_type=F32)
            if k != 2:
                r += sums[g]
            if k != 0:
                sums[g] = r
            else:
                proj[g] = jnp.where(diag, r, 0.0).astype(BF)
            return 0

        lax.fori_loop(0, PAD // 8, project, 0, unroll=2)
    for c in places:
        c.wait()
    tab_copy.wait()
    (inv_copy,) = starts(pltpu.make_async_copy(inv_r, inv_s, csem.at[10]))

    out1 = []
    for q in range(PARTS // 2):
        cols = slice(WIDE * q, WIDE * (q + 1))

        def far(g, _, cols=cols):
            w = left[pl.ds(8 * g, 8), :, cols].reshape(256, WIDE)
            t = jnp.dot(proj[g], w, preferred_element_type=F32)
            term[pl.ds(8 * g, 8)] = t.reshape(8, RHS, WIDE)
            return 0

        lax.fori_loop(0, PAD // 8, far, 0, unroll=4)
        for n in range(NEAR):
            term[FAR + n] = lax.dot_general(
                jnp.concatenate([cluster(near_src[n], k) for k in range(3)], axis=1), near[n, cols, :], (((1,), (1,)), ((), ())), preferred_element_type=F32
            )

        def scan(i, carry):
            value, before = carry
            row = tab_s[1, i]
            value = value * (row == before).astype(F32) + term[tab_s[0, i]]
            cum[i] = value.astype(BF)
            return value, row

        lax.fori_loop(0, PAD, scan, (jnp.zeros((RHS, WIDE), F32), jnp.int32(-1)), unroll=8)

        for h in range(2):
            first, second = AXES[h]
            part = slice(THIN * h, THIN * (h + 1))
            out1.append([])
            for d in (1, 3, 2, 0):

                def load(i, _, q=2 * q + h, d=d, first=first, second=second, part=part):
                    w, t = i // 8, i % 8
                    value = cum[tab_s[2, moved({first: d, second: w})[1] * 8 + t], :, part]
                    if d == 0:
                        recv[q][0, w, t] = value
                    else:
                        send[q, d - 1, w, t] = value
                    return 0

                lax.fori_loop(0, 32, load, 0, unroll=8)
                if d:
                    out1[-1] += starts(remote(
                        send.at[2 * q + h, d - 1], recv[2 * q + h].at[4 - d, :, pl.ds(0, SLOTS)],
                        o1s.at[2 * q + h, d - 1], o1r.at[2 * q + h, d - 1], moved({first: d}),
                    ))

    inv_copy.wait()
    out2 = []
    for q in range(PARTS):
        h = q % 2
        first, second = AXES[h]
        for c in out1[q]:
            c.wait_recv()
        out2.append([])
        for d in (1, 3, 2, 0):

            def add(r, _, q=q, h=h, d=d, second=second):
                at = moved({second: d})[1] * 16 + r
                total = recv[q][0, d, inv_s[h, 0, 0, at]].astype(F32)
                for e in range(1, 4):
                    total += recv[q][e, d, inv_s[h, e, 0, at]].astype(F32)
                if d == 0:
                    out_v[q, r] = total
                else:
                    fold[q, d - 1, r] = total.astype(BF)
                return 0

            lax.fori_loop(0, CL, add, 0, unroll=4)
            if d:
                out2[q] += starts(remote(
                    fold.at[q, d - 1], last.at[q, d - 1], o2s.at[q, d - 1], o2r.at[q, d - 1], moved({second: d})
                ))
    results = []
    for q in range(PARTS):
        for c in out2[q]:
            c.wait_recv()

        def finish(r, _, q=q):
            total = out_v[q, r]
            for e in range(3):
                total += last[q, e, r].astype(F32)
            out_v[q, r] = total
            return 0

        lax.fori_loop(0, CL, finish, 0, unroll=4)
        results += starts(pltpu.make_async_copy(out_v.at[q], out.at[:, :, pl.ds(THIN * q, THIN)], osem.at[q]))

    for c in slots1 + sum(stage1, []) + sum(stage2, []) + sum(stage3, []) + sum(out1, []) + sum(out2, []):
        c.wait_send()
    for c in results:
        c.wait()


def local(xin, send_slot, near_blocks, near_row, near_src, far_left, far_right, far_row, far_src):
    hbm = pl.BlockSpec(memory_space=pl.ANY)
    widths = [w for _, w in COLS]
    dma, vmem, smem = pltpu.SemaphoreType.DMA, pltpu.VMEM, pltpu.SMEM
    scratch = [vmem((CL, RHS, LEAF), BF)]
    scratch += [smem((NEAR,), I32), smem((NEAR,), I32), smem((FAR,), I32), smem((FAR,), I32)]
    scratch += [vmem((3, 3, 1, 128), I32), smem((1, 128), I32), smem((3, 3, 1, 128), I32)]
    scratch += [vmem((3, CL, RHS, w), BF) for w in widths]
    scratch += [vmem((3, 4, 4, 2, RHS, w), BF) for w in widths]
    scratch += [vmem((4, 4, 4, 2, RHS, w), BF) for w in widths]
    scratch += [vmem((4, 2, 4, 4, RHS, w), BF) for w in widths]
    scratch += [
        vmem((NEAR, LEAF, LEAF), BF),
        vmem((PAD, RANK, LEAF), BF),
        vmem((PAD, RANK, LEAF), BF),
        vmem((PAD, 256), I32),
        vmem((8, 256), I32),
        smem((8, 256), I32),
        vmem((1, 256), I32),
        vmem((2, 4, 1, 256), I32),
        smem((2, 4, 1, 256), I32),
        vmem((PAD // 8, 128, 256), F32),
        vmem((PAD // 8, 128, 256), BF),
        vmem((PAD, RHS, WIDE), F32),
        vmem((PAD, RHS, WIDE), BF),
        vmem((PARTS, 3, 4, SLOTS, RHS, THIN), BF),
        *[vmem((4, 4, SLOTS + 1, RHS, THIN), BF)] * PARTS,
        vmem((PARTS, 3, CL, RHS, THIN), BF),
        vmem((PARTS, 3, CL, RHS, THIN), BF),
        vmem((PARTS, CL, RHS, THIN), F32),
    ]
    scratch += [dma((3,)), dma((11,)), dma((3, 2))] + [dma((3, 3))] * 4 + [dma((3, 2, 3))] * 2 + [dma((3, 2, 7))] * 2
    scratch += [dma((2, 3))] * 2 + [dma((PARTS, 3))] * 4 + [dma((PARTS,))]
    return pl.pallas_call(
        kernel,
        out_shape=jax.ShapeDtypeStruct((CL, RHS, LEAF), F32),
        in_specs=[hbm] * 9,
        out_specs=hbm,
        scratch_shapes=scratch,
        compiler_params=pltpu.CompilerParams(
            collective_id=0, has_side_effects=True, vmem_limit_bytes=60 << 20
        ),
        cost_estimate=pl.CostEstimate(flops=800_000_000, bytes_accessed=26_000_000, transcendentals=0),
        name="hmatrix",
    )(xin, send_slot, near_row, near_src, far_row, far_src, near_blocks, far_left, far_right)


def solution(mesh):
    both = ("sfc", "blk")
    placed = (
        P(both, None, None), P(both, None), P(both, None, None), P(both), P(both),
        P(both, None, None), P(both, None, None), P(both), P(both),
    )
    return jax.shard_map(local, mesh=mesh, in_specs=placed, out_specs=P(both, None, None), check_vma=False)
```

```python
import functools

import jax
import jax.numpy as jnp
from jax import lax
from jax.experimental import pallas as pl
from jax.experimental.pallas import tpu as pltpu
from jax.sharding import PartitionSpec as P

MESH = pl.DeviceIdType.MESH
BF = jnp.bfloat16
F32 = jnp.float32
I32 = jnp.int32
CL, RHS, LEAF, RANK = 16, 16, 1024, 32
NEAR, FAR, SLOTS = 2, 156, 8
ALL = NEAR + FAR
PAD = 160
PARTS = 8
THIN = LEAF // PARTS
WIDE = 2 * THIN
COLS = ((0, 384), (384, 384), (768, 256))
ORDER = ((0, 1, 2), (1, 2, 0), (2, 0, 1))
AXES = ((1, 2), (2, 1))


def kernel(
    xin, slots_in, near_row_in, near_src_in, far_row_in, far_src_in, near_hbm, left_hbm, right_hbm,
    out,
    x_v, near_row, near_src, far_row, far_src, slot_v, slot_o, slot_s,
    g01, g02, g03, g11, g12, g13, g21, g22, g23, t0, t1, t2, m0, m1, m2, i0, i1, i2,
    near, left, right, keys, tab_v, tab_s, inv_v, inv_r, inv_s,
    proj, term, cum, send, r0, r1, r2, r3, r4, r5, r6, r7, fold, last, out_v,
    wsem, csem, ksem, s1s, s1r, sls, slr, s2s, s2r, s3s, s3r, ivs, ivr, o1s, o1r, o2s, o2r,
):
    sfc, blk = lax.axis_index("sfc"), lax.axis_index("blk")
    core = sfc % 2
    pos = (sfc // 2, blk // 4, blk % 4)

    def moved(steps, flip=0):
        p = [(pos[a] + steps.get(a, 0)) % 4 for a in range(3)]
        return p[0] * 2 + (core + flip) % 2, p[1] * 4 + p[2]

    def remote(src, dst, ssem, rsem, to):
        return pltpu.make_async_remote_copy(
            src_ref=src, dst_ref=dst, send_sem=ssem, recv_sem=rsem, device_id=to, device_id_type=MESH
        )

    def starts(*copies):
        for c in copies:
            c.start()
        return list(copies)

    barrier = pltpu.get_barrier_semaphore()
    peers = [moved({}, 1)] + [moved({a: d}, f) for a in range(3) for d in range(1, 4) for f in range(2)]
    for to in peers:
        pl.semaphore_signal(barrier, inc=1, device_id=to, device_id_type=MESH)
    own_x, own_slot = starts(
        pltpu.make_async_copy(xin, x_v, csem.at[0]),
        pltpu.make_async_copy(slots_in, slot_o, csem.at[1]),
    )
    index = starts(
        pltpu.make_async_copy(near_row_in, near_row, csem.at[2]),
        pltpu.make_async_copy(near_src_in, near_src, csem.at[3]),
        pltpu.make_async_copy(far_row_in, far_row, csem.at[4]),
        pltpu.make_async_copy(far_src_in, far_src, csem.at[5]),
    )
    right[FAR:PAD] = jnp.zeros((PAD - FAR, RANK, LEAF), BF)
    left[FAR:PAD] = jnp.zeros((PAD - FAR, RANK, LEAF), BF)

    recv = (r0, r1, r2, r3, r4, r5, r6, r7)

    def clear(i, _):
        for buffer in recv:
            buffer[i // 4, i % 4, SLOTS] = jnp.zeros((RHS, THIN), BF)
        return 0

    lax.fori_loop(0, 16, clear, 0)
    own_x.wait()
    own_slot.wait()
    pl.semaphore_wait(barrier, len(peers))

    got = ((None, g01, g02, g03), (None, g11, g12, g13), (None, g21, g22, g23))
    stage1, passed, slots1 = [[], [], []], [[], [], []], []
    for k in range(3):
        for d in (1, 3, 2):
            to = moved({ORDER[k][0]: d})
            slots1 += starts(remote(slots_in, slot_v.at[k, 3 - d], sls.at[k, d - 1], slr.at[k, d - 1], to))
    for d in (1, 3):
        for k in (2, 1, 0):
            lo, wide = COLS[k]
            stage1[k] += starts(remote(
                x_v.at[:, :, pl.ds(lo, wide)], got[k][4 - d],
                s1s.at[k, d - 1], s1r.at[k, d - 1], moved({ORDER[k][0]: d}),
            ))

    pick, mid = (t0, t1, t2), (m0, m1, m2)
    stage2 = [[], [], []]

    def wanted(k, a, c, f, d):
        where = moved({ORDER[k][1]: d, ORDER[k][2]: c}, f)
        return where[0] * 16 + where[1]

    def choose(k, d, a):
        lo, wide = COLS[k]

        def put(i, _):
            c, f = i // 2, i % 2
            if a == 0:
                v = x_v[slot_o[0, wanted(k, a, c, f, d)], :, lo : lo + wide]
            else:
                v = got[k][a][slot_s[k, a - 1, 0, wanted(k, a, c, f, d)]]
            if d:
                pick[k][d - 1, a, c, f] = v
            elif k == 2:
                mid[k][0, a, c, f] = v
            else:
                mid[k][a, 0, c, f] = v
            return 0

        lax.fori_loop(0, 8, put, 0, unroll=True)

    def pass_on(k, d, a):
        choose(k, d, a)
        dst = mid[k].at[4 - d, a] if k == 2 else mid[k].at[a, 4 - d]
        stage2[k] += starts(remote(
            pick[k].at[d - 1, a], dst, s2s.at[k, a, d - 1], s2r.at[k, a, d - 1], moved({ORDER[k][1]: d})
        ))

    for d in (1, 3, 2):
        for k in (2, 1, 0):
            pass_on(k, d, 0)
    weights = starts(
        pltpu.make_async_copy(right_hbm, right.at[pl.ds(0, FAR)], wsem.at[0]),
        pltpu.make_async_copy(left_hbm, left.at[pl.ds(0, FAR)], wsem.at[1]),
        pltpu.make_async_copy(near_hbm, near, wsem.at[2]),
    )
    for c in index:
        c.wait()

    def fill_far(j, _):
        keys[pl.ds(j, 1), :] = jnp.full((1, 256), far_row[j], I32)
        return 0

    lax.fori_loop(0, FAR, fill_far, 0, unroll=4)
    for j in range(NEAR):
        keys[FAR + j : FAR + j + 1, :] = jnp.full((1, 256), near_row[j], I32)
    keys[ALL:PAD, :] = jnp.full((PAD - ALL, 256), 300, I32)
    row_c = keys[...]
    down = lax.broadcasted_iota(I32, (PAD, 256), 0)
    lane = lax.broadcasted_iota(I32, (PAD, 256), 1)
    row_r = jnp.sum(jnp.where(down == lane, row_c, 0), axis=0, keepdims=True)
    real = lane < PAD
    same = real & (row_r == row_c)
    less = real & (row_r < row_c)
    first_r = jnp.sum(jnp.where(same & (down < lane), 1, 0), axis=0, keepdims=True) == 0
    place = jnp.sum(jnp.where(less | (same & (lane < down)), 1, 0), axis=1, keepdims=True)
    final = jnp.sum(jnp.where(less | same, 1, 0), axis=1, keepdims=True) - 1
    slot = jnp.sum(jnp.where(less & first_r, 1, 0), axis=1, keepdims=True)
    here = place == lane
    tab_v[0:1, :] = jnp.sum(jnp.where(here, down, 0), axis=0, keepdims=True)
    tab_v[1:2, :] = jnp.sum(jnp.where(here, row_c, 0), axis=0, keepdims=True)
    tab_v[2:3, :] = jnp.max(jnp.where(slot == lane, final, 0), axis=0, keepdims=True)
    seat = jnp.max(jnp.where(row_c == lane, 8 - (slot & 7), 0), axis=0, keepdims=True)
    inv_v[0:1, :] = 8 - seat
    (tab_copy,) = starts(pltpu.make_async_copy(tab_v, tab_s, csem.at[7]))
    places = []
    for h in range(2):
        for d in range(1, 4):
            places += starts(remote(
                inv_v, inv_r.at[h, 4 - d], ivs.at[h, d - 1], ivr.at[h, d - 1], moved({AXES[h][0]: d})
            ))
        places += starts(pltpu.make_async_copy(inv_v, inv_r.at[h, 0], csem.at[8 + h]))

    inc = (i0, i1, i2)

    stage3, own3 = [[], [], []], [[], [], []]

    def deliver(k, group):
        part = 0 if group == 0 else pl.ds(1, 3)
        for d in (1, 3, 2, 0):
            e = (4 - d) % 4
            for f in range(2):
                if k == 2:
                    src, dst = mid[k].at[part, :, d, f], inc[k].at[part, f, e]
                elif k == 1:
                    src, dst = mid[k].at[:, part, d, f], inc[k].at[e, f, :, part]
                else:
                    src, dst = mid[k].at[:, part, d, f], inc[k].at[:, f, part, e]
                if d == 0 and f == 0:
                    own3[k].extend(starts(pltpu.make_async_copy(src, dst, ksem.at[k, group])))
                else:
                    n = d * 2 + f - 1
                    stage3[k].extend(starts(remote(
                        src, dst, s3s.at[k, group, n], s3r.at[k, group, n], moved({ORDER[k][2]: d}, f)
                    )))

    for k in (2, 1, 0):
        for c in stage1[k]:
            c.wait_recv()
        for n, (d, a) in enumerate(((1, 3), (3, 1))):
            half = pl.ds(8 * n, 8)
            passed[k] += starts(remote(
                got[k][a].at[half], got[k][2].at[half],
                s1s.at[k, n + 3], s1r.at[k, n + 3], moved({ORDER[k][0]: d}),
            ))
    for c in slots1:
        c.wait_recv()
    (slot_copy,) = starts(pltpu.make_async_copy(slot_v, slot_s, csem.at[6]))

    slot_copy.wait()
    for a in (1, 3, 2):
        for k in (2, 1, 0):
            if a == 2:
                for c in passed[k]:
                    c.wait_recv()
            for d in (1, 3, 2):
                pass_on(k, d, a)
    for k in (2, 1, 0):
        for a in range(4):
            choose(k, 0, a)
        deliver(k, 0)
    for k in (2, 1, 0):
        for c in stage2[k]:
            c.wait_recv()
        deliver(k, 1)

    def cluster(s, k):
        return inc[k][
            ((s >> 5) - pos[0]) & 3, ((s >> 4) - core) & 1, ((s >> 2) - pos[1]) & 3, (s - pos[2]) & 3
        ]

    diag = lax.broadcasted_iota(I32, (128, 256), 0) // 16 == lax.broadcasted_iota(I32, (128, 256), 1) // 32
    for c in weights:
        c.wait()
    for k in (2, 1, 0):
        for c in stage3[k]:
            c.wait_recv()
        for c in own3[k]:
            c.wait()

        def project(g, _, k=k):
            lo, wide = COLS[k]
            x = jnp.concatenate([cluster(far_src[jnp.minimum(8 * g + e, FAR - 1)], k) for e in range(8)], axis=0)
            w = right[pl.ds(8 * g, 8), :, lo : lo + wide].reshape(256, wide)
            r = lax.dot_general(x, w, (((1,), (1,)), ((), ())), preferred_element_type=F32)
            if k != 2:
                r += term[pl.ds(8 * g, 8)].reshape(128, 256)
            if k != 0:
                term[pl.ds(8 * g, 8)] = r.reshape(8, RHS, 256)
            else:
                proj[g] = jnp.where(diag, r, 0.0).astype(BF)
            return 0

        lax.fori_loop(0, PAD // 8, project, 0, unroll=20)
    for c in places:
        c.wait()
    tab_copy.wait()
    (inv_copy,) = starts(pltpu.make_async_copy(inv_r, inv_s, csem.at[10]))

    out1 = []
    for q in range(PARTS // 2):
        cols = slice(WIDE * q, WIDE * (q + 1))

        def far(g, _, cols=cols):
            w = left[pl.ds(8 * g, 8), :, cols].reshape(256, WIDE)
            t = jnp.dot(proj[g], w, preferred_element_type=F32)
            term[pl.ds(8 * g, 8)] = t.reshape(8, RHS, WIDE)
            return 0

        lax.fori_loop(0, PAD // 8, far, 0, unroll=20)
        for n in range(NEAR):
            term[FAR + n] = lax.dot_general(
                jnp.concatenate([cluster(near_src[n], k) for k in range(3)], axis=1), near[n, cols, :], (((1,), (1,)), ((), ())), preferred_element_type=F32
            )

        def scan(i, carry):
            value, before = carry
            row = tab_s[1, i]
            value = value * (row == before).astype(F32) + term[tab_s[0, i]]
            cum[i] = value.astype(BF)
            return value, row

        lax.fori_loop(0, PAD, scan, (jnp.zeros((RHS, WIDE), F32), jnp.int32(-1)), unroll=16)

        for h in range(2):
            first, second = AXES[h]
            part = slice(THIN * h, THIN * (h + 1))
            out1.append([])
            for d in (1, 3, 2, 0):

                def load(i, _, q=2 * q + h, d=d, first=first, second=second, part=part):
                    w, t = i // 8, i % 8
                    value = cum[tab_s[2, moved({first: d, second: w})[1] * 8 + t], :, part]
                    if d == 0:
                        recv[q][0, w, t] = value
                    else:
                        send[q, d - 1, w, t] = value
                    return 0

                lax.fori_loop(0, 32, load, 0, unroll=8)
                if d:
                    out1[-1] += starts(remote(
                        send.at[2 * q + h, d - 1], recv[2 * q + h].at[4 - d, :, pl.ds(0, SLOTS)],
                        o1s.at[2 * q + h, d - 1], o1r.at[2 * q + h, d - 1], moved({first: d}),
                    ))

    inv_copy.wait()
    out2 = []
    for q in range(PARTS):
        h = q % 2
        first, second = AXES[h]
        for c in out1[q]:
            c.wait_recv()
        out2.append([])
        for d in (1, 3, 2, 0):

            def add(r, _, q=q, h=h, d=d, second=second):
                at = moved({second: d})[1] * 16 + r
                total = recv[q][0, d, inv_s[h, 0, 0, at]].astype(F32)
                for e in range(1, 4):
                    total += recv[q][e, d, inv_s[h, e, 0, at]].astype(F32)
                if d == 0:
                    out_v[q, r] = total
                else:
                    fold[q, d - 1, r] = total.astype(BF)
                return 0

            lax.fori_loop(0, CL, add, 0, unroll=4)
            if d:
                out2[q] += starts(remote(
                    fold.at[q, d - 1], last.at[q, d - 1], o2s.at[q, d - 1], o2r.at[q, d - 1], moved({second: d})
                ))
    for q in range(PARTS):
        for c in out2[q]:
            c.wait_recv()

        def finish(r, _, q=q):
            total = out_v[q, r]
            for e in range(3):
                total += last[q, e, r].astype(F32)
            out[r, :, THIN * q : THIN * (q + 1)] = total
            return 0

        lax.fori_loop(0, CL, finish, 0, unroll=4)

    for c in slots1 + sum(stage1, []) + sum(passed, []) + sum(stage2, []) + sum(stage3, []) + sum(out1, []) + sum(out2, []):
        c.wait_send()


def local(xin, send_slot, near_blocks, near_row, near_src, far_left, far_right, far_row, far_src):
    hbm = pl.BlockSpec(memory_space=pl.ANY)
    widths = [w for _, w in COLS]
    dma, vmem, smem = pltpu.SemaphoreType.DMA, pltpu.VMEM, pltpu.SMEM
    scratch = [vmem((CL, RHS, LEAF), BF)]
    scratch += [smem((NEAR,), I32), smem((NEAR,), I32), smem((FAR,), I32), smem((FAR,), I32)]
    scratch += [vmem((3, 3, 1, 128), I32), smem((1, 128), I32), smem((3, 3, 1, 128), I32)]
    scratch += [vmem((CL, RHS, w), BF) for w in widths for _ in range(3)]
    scratch += [vmem((3, 4, 4, 2, RHS, w), BF) for w in widths]
    scratch += [vmem((4, 4, 4, 2, RHS, w), BF) for w in widths]
    scratch += [vmem((4, 2, 4, 4, RHS, w), BF) for w in widths]
    scratch += [
        vmem((NEAR, LEAF, LEAF), BF),
        vmem((PAD, RANK, LEAF), BF),
        vmem((PAD, RANK, LEAF), BF),
        vmem((PAD, 256), I32),
        vmem((8, 256), I32),
        smem((8, 256), I32),
        vmem((1, 256), I32),
        vmem((2, 4, 1, 256), I32),
        smem((2, 4, 1, 256), I32),
        vmem((PAD // 8, 128, 256), BF),
        vmem((PAD, RHS, WIDE), F32),
        vmem((PAD, RHS, WIDE), BF),
        vmem((PARTS, 3, 4, SLOTS, RHS, THIN), BF),
        *[vmem((4, 4, SLOTS + 1, RHS, THIN), BF)] * PARTS,
        vmem((PARTS, 3, CL, RHS, THIN), BF),
        vmem((PARTS, 3, CL, RHS, THIN), BF),
        vmem((PARTS, CL, RHS, THIN), F32),
    ]
    scratch += [dma((3,)), dma((11,)), dma((3, 2))] + [dma((3, 5))] * 2 + [dma((3, 3))] * 2 + [dma((3, 4, 3))] * 2 + [dma((3, 2, 7))] * 2
    scratch += [dma((2, 3))] * 2 + [dma((PARTS, 3))] * 4
    return pl.pallas_call(
        kernel,
        out_shape=pltpu.VMEM((CL, RHS, LEAF), F32),
        in_specs=[hbm] * 9,
        out_specs=pl.BlockSpec(memory_space=pltpu.VMEM),
        scratch_shapes=scratch,
        compiler_params=pltpu.CompilerParams(
            collective_id=0, has_side_effects=True, vmem_limit_bytes=56 << 20
        ),
        cost_estimate=pl.CostEstimate(flops=800_000_000, bytes_accessed=26_000_000, transcendentals=0),
        name="hmatrix",
    )(xin, send_slot, near_row, near_src, far_row, far_src, near_blocks, far_left, far_right)


def solution(mesh):
    both = ("sfc", "blk")
    placed = (
        P(both, None, None), P(both, None), P(both, None, None), P(both), P(both),
        P(both, None, None), P(both, None, None), P(both), P(both),
    )
    return jax.shard_map(local, mesh=mesh, in_specs=placed, out_specs=P(both, None, None), check_vma=False)
```

```python
import functools

import jax
import jax.numpy as jnp
from jax import lax
from jax.experimental import pallas as pl
from jax.experimental.pallas import tpu as pltpu
from jax.sharding import PartitionSpec as P

MESH = pl.DeviceIdType.MESH
BF = jnp.bfloat16
F32 = jnp.float32
I32 = jnp.int32
CL, RHS, LEAF, RANK = 16, 16, 1024, 32
NEAR, FAR, SLOTS = 2, 156, 8
ALL = NEAR + FAR
PAD = 160
PARTS = 8
THIN = LEAF // PARTS
WIDE = 2 * THIN
COLS = ((0, 384), (384, 384), (768, 256))
ORDER = ((0, 1, 2), (1, 2, 0), (2, 0, 1))
AXES = ((1, 2), (2, 1))


def kernel(
    xin, slots_in, near_row_in, near_src_in, far_row_in, far_src_in, near_hbm, left_hbm, right_hbm,
    out,
    x_v, near_row, near_src, far_row, far_src, slot_v, slot_o, slot_s,
    g01, g02, g03, g11, g12, g13, g21, g22, g23, t0, t1, t2, m0, m1, m2, i0, i1, i2,
    near, left, right, keys, tab_v, tab_s, inv_v, inv_r, inv_s,
    proj, term, cum, send, r0, r1, r2, r3, r4, r5, r6, r7, fold, last, out_v,
    wsem, csem, ksem, s1s, s1r, sls, slr, s2s, s2r, s3s, s3r, ivs, ivr, o1s, o1r, o2s, o2r,
):
    sfc, blk = lax.axis_index("sfc"), lax.axis_index("blk")
    core = sfc % 2
    pos = (sfc // 2, blk // 4, blk % 4)

    def moved(steps, flip=0):
        p = [(pos[a] + steps.get(a, 0)) % 4 for a in range(3)]
        return p[0] * 2 + (core + flip) % 2, p[1] * 4 + p[2]

    def remote(src, dst, ssem, rsem, to):
        return pltpu.make_async_remote_copy(
            src_ref=src, dst_ref=dst, send_sem=ssem, recv_sem=rsem, device_id=to, device_id_type=MESH
        )

    def starts(*copies):
        for c in copies:
            c.start()
        return list(copies)

    barrier = pltpu.get_barrier_semaphore()
    peers = [moved({}, 1)] + [moved({a: d}, f) for a in range(3) for d in range(1, 4) for f in range(2)]
    for to in peers:
        pl.semaphore_signal(barrier, inc=1, device_id=to, device_id_type=MESH)
    own_x, own_slot = starts(
        pltpu.make_async_copy(xin, x_v, csem.at[0]),
        pltpu.make_async_copy(slots_in, slot_o, csem.at[1]),
    )
    index = starts(
        pltpu.make_async_copy(near_row_in, near_row, csem.at[2]),
        pltpu.make_async_copy(near_src_in, near_src, csem.at[3]),
        pltpu.make_async_copy(far_row_in, far_row, csem.at[4]),
        pltpu.make_async_copy(far_src_in, far_src, csem.at[5]),
    )
    right[FAR:PAD] = jnp.zeros((PAD - FAR, RANK, LEAF), BF)
    left[FAR:PAD] = jnp.zeros((PAD - FAR, RANK, LEAF), BF)

    recv = (r0, r1, r2, r3, r4, r5, r6, r7)

    def clear(i, _):
        for buffer in recv:
            buffer[i // 4, i % 4, SLOTS] = jnp.zeros((RHS, THIN), BF)
        return 0

    lax.fori_loop(0, 16, clear, 0)
    own_x.wait()
    own_slot.wait()
    pl.semaphore_wait(barrier, len(peers))

    got = ((None, g01, g02, g03), (None, g11, g12, g13), (None, g21, g22, g23))
    stage1, passed, slots1 = [[], [], []], [[], [], []], []
    for k in range(3):
        for d in (1, 3, 2):
            to = moved({ORDER[k][0]: d})
            slots1 += starts(remote(slots_in, slot_v.at[k, 3 - d], sls.at[k, d - 1], slr.at[k, d - 1], to))
    for d in (1, 3):
        for k in (2, 1, 0):
            lo, wide = COLS[k]
            stage1[k] += starts(remote(
                x_v.at[:, :, pl.ds(lo, wide)], got[k][4 - d],
                s1s.at[k, d - 1], s1r.at[k, d - 1], moved({ORDER[k][0]: d}),
            ))

    pick, mid = (t0, t1, t2), (m0, m1, m2)
    stage2 = [[], [], []]

    def wanted(k, a, c, f, d):
        where = moved({ORDER[k][1]: d, ORDER[k][2]: c}, f)
        return where[0] * 16 + where[1]

    def choose(k, d, a):
        lo, wide = COLS[k]

        def put(i, _):
            c, f = i // 2, i % 2
            if a == 0:
                v = x_v[slot_o[0, wanted(k, a, c, f, d)], :, lo : lo + wide]
            else:
                v = got[k][a][slot_s[k, a - 1, 0, wanted(k, a, c, f, d)]]
            if d:
                pick[k][d - 1, a, c, f] = v
            elif k == 2:
                mid[k][0, a, c, f] = v
            else:
                mid[k][a, 0, c, f] = v
            return 0

        lax.fori_loop(0, 8, put, 0, unroll=True)

    def pass_on(k, d, a):
        choose(k, d, a)
        dst = mid[k].at[4 - d, a] if k == 2 else mid[k].at[a, 4 - d]
        stage2[k] += starts(remote(
            pick[k].at[d - 1, a], dst, s2s.at[k, a, d - 1], s2r.at[k, a, d - 1], moved({ORDER[k][1]: d})
        ))

    for d in (1, 3, 2):
        for k in (2, 1, 0):
            pass_on(k, d, 0)
    weights = starts(
        pltpu.make_async_copy(right_hbm, right.at[pl.ds(0, FAR)], wsem.at[0]),
        pltpu.make_async_copy(left_hbm, left.at[pl.ds(0, FAR)], wsem.at[1]),
        pltpu.make_async_copy(near_hbm, near, wsem.at[2]),
    )
    for c in index:
        c.wait()

    def fill_far(j, _):
        keys[pl.ds(j, 1), :] = jnp.full((1, 256), far_row[j], I32)
        return 0

    lax.fori_loop(0, FAR, fill_far, 0, unroll=12)
    for j in range(NEAR):
        keys[FAR + j : FAR + j + 1, :] = jnp.full((1, 256), near_row[j], I32)
    keys[ALL:PAD, :] = jnp.full((PAD - ALL, 256), 300, I32)
    row_c = keys[...]
    down = lax.broadcasted_iota(I32, (PAD, 256), 0)
    lane = lax.broadcasted_iota(I32, (PAD, 256), 1)
    row_r = jnp.sum(jnp.where(down == lane, row_c, 0), axis=0, keepdims=True)
    real = lane < PAD
    same = real & (row_r == row_c)
    less = real & (row_r < row_c)
    first_r = jnp.sum(jnp.where(same & (down < lane), 1, 0), axis=0, keepdims=True) == 0
    place = jnp.sum(jnp.where(less | (same & (lane < down)), 1, 0), axis=1, keepdims=True)
    final = jnp.sum(jnp.where(less | same, 1, 0), axis=1, keepdims=True) - 1
    slot = jnp.sum(jnp.where(less & first_r, 1, 0), axis=1, keepdims=True)
    here = place == lane
    tab_v[0:1, :] = jnp.sum(jnp.where(here, down, 0), axis=0, keepdims=True)
    tab_v[1:2, :] = jnp.sum(jnp.where(here, row_c, 0), axis=0, keepdims=True)
    tab_v[2:3, :] = jnp.max(jnp.where(slot == lane, final, 0), axis=0, keepdims=True)
    seat = jnp.max(jnp.where(row_c == lane, 8 - (slot & 7), 0), axis=0, keepdims=True)
    inv_v[0:1, :] = 8 - seat
    (tab_copy,) = starts(pltpu.make_async_copy(tab_v, tab_s, csem.at[7]))
    places = []
    for h in range(2):
        for d in range(1, 4):
            places += starts(remote(
                inv_v, inv_r.at[h, 4 - d], ivs.at[h, d - 1], ivr.at[h, d - 1], moved({AXES[h][0]: d})
            ))
        places += starts(pltpu.make_async_copy(inv_v, inv_r.at[h, 0], csem.at[8 + h]))

    inc = (i0, i1, i2)

    stage3, own3 = [[], [], []], [[], [], []]

    def deliver(k, group):
        part = 0 if group == 0 else pl.ds(1, 3)
        for d in (1, 3, 2, 0):
            e = (4 - d) % 4
            for f in range(2):
                if k == 2:
                    src, dst = mid[k].at[part, :, d, f], inc[k].at[part, f, e]
                elif k == 1:
                    src, dst = mid[k].at[:, part, d, f], inc[k].at[e, f, :, part]
                else:
                    src, dst = mid[k].at[:, part, d, f], inc[k].at[:, f, part, e]
                if d == 0 and f == 0:
                    own3[k].extend(starts(pltpu.make_async_copy(src, dst, ksem.at[k, group])))
                else:
                    n = d * 2 + f - 1
                    stage3[k].extend(starts(remote(
                        src, dst, s3s.at[k, group, n], s3r.at[k, group, n], moved({ORDER[k][2]: d}, f)
                    )))

    for k in (2, 1, 0):
        for c in stage1[k]:
            c.wait_recv()
        for n, (d, a) in enumerate(((1, 3), (3, 1))):
            half = pl.ds(8 * n, 8)
            passed[k] += starts(remote(
                got[k][a].at[half], got[k][2].at[half],
                s1s.at[k, n + 3], s1r.at[k, n + 3], moved({ORDER[k][0]: d}),
            ))
    for c in slots1:
        c.wait_recv()
    (slot_copy,) = starts(pltpu.make_async_copy(slot_v, slot_s, csem.at[6]))

    slot_copy.wait()
    for a in (1, 3, 2):
        for k in (2, 1, 0):
            if a == 2:
                for c in passed[k]:
                    c.wait_recv()
            for d in (1, 3, 2):
                pass_on(k, d, a)
    for k in (2, 1, 0):
        for a in range(4):
            choose(k, 0, a)
        deliver(k, 0)
    for k in (2, 1, 0):
        for c in stage2[k]:
            c.wait_recv()
        deliver(k, 1)

    def cluster(s, k):
        return inc[k][
            ((s >> 5) - pos[0]) & 3, ((s >> 4) - core) & 1, ((s >> 2) - pos[1]) & 3, (s - pos[2]) & 3
        ]

    diag = lax.broadcasted_iota(I32, (128, 256), 0) // 16 == lax.broadcasted_iota(I32, (128, 256), 1) // 32
    for c in weights:
        c.wait()
    for k in (2, 1, 0):
        for c in stage3[k]:
            c.wait_recv()
        for c in own3[k]:
            c.wait()

        def project(g, _, k=k):
            lo, wide = COLS[k]
            x = jnp.concatenate([cluster(far_src[jnp.minimum(8 * g + e, FAR - 1)], k) for e in range(8)], axis=0)
            w = right[pl.ds(8 * g, 8), :, lo : lo + wide].reshape(256, wide)
            r = lax.dot_general(x, w, (((1,), (1,)), ((), ())), preferred_element_type=F32)
            if k != 2:
                r += term[pl.ds(8 * g, 8)].reshape(128, 256)
            if k != 0:
                term[pl.ds(8 * g, 8)] = r.reshape(8, RHS, 256)
            else:
                proj[g] = jnp.where(diag, r, 0.0).astype(BF)
            return 0

        lax.fori_loop(0, PAD // 8, project, 0, unroll=20)
    for c in places:
        c.wait()
    tab_copy.wait()
    (inv_copy,) = starts(pltpu.make_async_copy(inv_r, inv_s, csem.at[10]))

    out1 = []
    for q in range(PARTS // 2):
        cols = slice(WIDE * q, WIDE * (q + 1))

        def far(g, _, cols=cols):
            w = left[pl.ds(8 * g, 8), :, cols].reshape(256, WIDE)
            t = jnp.dot(proj[g], w, preferred_element_type=F32)
            term[pl.ds(8 * g, 8)] = t.reshape(8, RHS, WIDE)
            return 0

        lax.fori_loop(0, PAD // 8, far, 0, unroll=20)
        for n in range(NEAR):
            term[FAR + n] = lax.dot_general(
                jnp.concatenate([cluster(near_src[n], k) for k in range(3)], axis=1), near[n, cols, :], (((1,), (1,)), ((), ())), preferred_element_type=F32
            )

        def scan(i, carry):
            value, before = carry
            row = tab_s[1, i]
            value = value * (row == before).astype(F32) + term[tab_s[0, i]]
            cum[i] = value.astype(BF)
            return value, row

        lax.fori_loop(0, PAD, scan, (jnp.zeros((RHS, WIDE), F32), jnp.int32(-1)), unroll=32)

        for h in range(2):
            first, second = AXES[h]
            part = slice(THIN * h, THIN * (h + 1))
            out1.append([])
            for d in (1, 3, 2, 0):

                def load(i, _, q=2 * q + h, d=d, first=first, second=second, part=part):
                    w, t = i // 8, i % 8
                    value = cum[tab_s[2, moved({first: d, second: w})[1] * 8 + t], :, part]
                    if d == 0:
                        recv[q][0, w, t] = value
                    else:
                        send[q, d - 1, w, t] = value
                    return 0

                lax.fori_loop(0, 32, load, 0, unroll=16)
                if d:
                    out1[-1] += starts(remote(
                        send.at[2 * q + h, d - 1], recv[2 * q + h].at[4 - d, :, pl.ds(0, SLOTS)],
                        o1s.at[2 * q + h, d - 1], o1r.at[2 * q + h, d - 1], moved({first: d}),
                    ))

    inv_copy.wait()
    out2 = []
    for q in range(PARTS):
        h = q % 2
        first, second = AXES[h]
        for c in out1[q]:
            c.wait_recv()
        out2.append([])
        for d in (1, 3, 2, 0):

            def add(r, _, q=q, h=h, d=d, second=second):
                at = moved({second: d})[1] * 16 + r
                total = recv[q][0, d, inv_s[h, 0, 0, at]].astype(F32)
                for e in range(1, 4):
                    total += recv[q][e, d, inv_s[h, e, 0, at]].astype(F32)
                if d == 0:
                    out_v[q, r] = total
                else:
                    fold[q, d - 1, r] = total.astype(BF)
                return 0

            lax.fori_loop(0, CL, add, 0, unroll=16)
            if d:
                out2[q] += starts(remote(
                    fold.at[q, d - 1], last.at[q, d - 1], o2s.at[q, d - 1], o2r.at[q, d - 1], moved({second: d})
                ))
    for q in range(PARTS):
        for c in out2[q]:
            c.wait_recv()

        def finish(r, _, q=q):
            total = out_v[q, r]
            for e in range(3):
                total += last[q, e, r].astype(F32)
            out[r, :, THIN * q : THIN * (q + 1)] = total
            return 0

        lax.fori_loop(0, CL, finish, 0, unroll=16)

    for c in slots1 + sum(stage1, []) + sum(passed, []) + sum(stage2, []) + sum(stage3, []) + sum(out1, []) + sum(out2, []):
        c.wait_send()


def local(xin, send_slot, near_blocks, near_row, near_src, far_left, far_right, far_row, far_src):
    hbm = pl.BlockSpec(memory_space=pl.ANY)
    widths = [w for _, w in COLS]
    dma, vmem, smem = pltpu.SemaphoreType.DMA, pltpu.VMEM, pltpu.SMEM
    scratch = [vmem((CL, RHS, LEAF), BF)]
    scratch += [smem((NEAR,), I32), smem((NEAR,), I32), smem((FAR,), I32), smem((FAR,), I32)]
    scratch += [vmem((3, 3, 1, 128), I32), smem((1, 128), I32), smem((3, 3, 1, 128), I32)]
    scratch += [vmem((CL, RHS, w), BF) for w in widths for _ in range(3)]
    scratch += [vmem((3, 4, 4, 2, RHS, w), BF) for w in widths]
    scratch += [vmem((4, 4, 4, 2, RHS, w), BF) for w in widths]
    scratch += [vmem((4, 2, 4, 4, RHS, w), BF) for w in widths]
    scratch += [
        vmem((NEAR, LEAF, LEAF), BF),
        vmem((PAD, RANK, LEAF), BF),
        vmem((PAD, RANK, LEAF), BF),
        vmem((PAD, 256), I32),
        vmem((8, 256), I32),
        smem((8, 256), I32),
        vmem((1, 256), I32),
        vmem((2, 4, 1, 256), I32),
        smem((2, 4, 1, 256), I32),
        vmem((PAD // 8, 128, 256), BF),
        vmem((PAD, RHS, WIDE), F32),
        vmem((PAD, RHS, WIDE), BF),
        vmem((PARTS, 3, 4, SLOTS, RHS, THIN), BF),
        *[vmem((4, 4, SLOTS + 1, RHS, THIN), BF)] * PARTS,
        vmem((PARTS, 3, CL, RHS, THIN), BF),
        vmem((PARTS, 3, CL, RHS, THIN), BF),
        vmem((PARTS, CL, RHS, THIN), F32),
    ]
    scratch += [dma((3,)), dma((11,)), dma((3, 2))] + [dma((3, 5))] * 2 + [dma((3, 3))] * 2 + [dma((3, 4, 3))] * 2 + [dma((3, 2, 7))] * 2
    scratch += [dma((2, 3))] * 2 + [dma((PARTS, 3))] * 4
    return pl.pallas_call(
        kernel,
        out_shape=pltpu.VMEM((CL, RHS, LEAF), F32),
        in_specs=[hbm] * 9,
        out_specs=pl.BlockSpec(memory_space=pltpu.VMEM),
        scratch_shapes=scratch,
        compiler_params=pltpu.CompilerParams(
            collective_id=0, has_side_effects=True, vmem_limit_bytes=56 << 20
        ),
        cost_estimate=pl.CostEstimate(flops=800_000_000, bytes_accessed=26_000_000, transcendentals=0),
        name="hmatrix",
    )(xin, send_slot, near_row, near_src, far_row, far_src, near_blocks, far_left, far_right)


def solution(mesh):
    both = ("sfc", "blk")
    placed = (
        P(both, None, None), P(both, None), P(both, None, None), P(both), P(both),
        P(both, None, None), P(both, None, None), P(both), P(both),
    )
    return jax.shard_map(local, mesh=mesh, in_specs=placed, out_specs=P(both, None, None), check_vma=False)
```
